32 devices in a mesh: groups: 2 (over x), tm: 8 (over z, y), sector: 2 (over core).
Axes of the slice: x: 2, y: 2, z: 4, core: 2. Of those that a mesh axis runs over, the one named last changes fastest.
Arguments:
- context: bfloat16 [16, 2, 512, 256], P(('groups', 'tm'), 'sector'), parts along dimension 0, may hold values from -6 to 6
- depth_weight: float32 [16, 2, 16, 512], P(('groups', 'tm'), 'sector'), parts along dimension 0, may hold values from 0 to 1
- cell_ids: int32 [2, 16, 512], P('sector'), may hold values from 0 to 4095
- time_embed: bfloat16 [8, 256], replicated, may hold values from -3 to 3
- norm_gain: float32 [2, 2, 256], replicated, may hold values from 0.1 to 1.9
- w_qkv: bfloat16 [2, 256, 768], replicated, may hold values from -15 to 15
- w_out: bfloat16 [2, 256, 256], replicated, may hold values from -0.375 to 0.375
- w_up: bfloat16 [2, 256, 1024], replicated, may hold values from -0.375 to 0.375
- w_down: bfloat16 [2, 1024, 256], replicated, may hold values from -0.1875 to 0.1875
- conv_weight: bfloat16 [3, 3, 256, 256], replicated, may hold values from -0.125 to 0.125
Outputs:
- bev_out: bfloat16 [16, 64, 64, 256], P(('groups', 'tm'), 'sector'), parts along dimension 0
The draws below stay inside these ranges and needn't reach their ends.
There are 2 independent parts, one for each index of `groups`. The reference program is written for one: setup_inputs(seed, part) draws one part's arguments, and reference() takes and returns one part's arrays. A program takes and returns all parts, laid end to end along the dimension named above; an argument that names none is the same for every part. Nothing has to cross between parts.
All inputs are finite; a program needn't handle non-finite values.
Results may differ from the reference program's by a relative error of at most 0.0079.
Values may be sent and summed in bfloat16 or wider, within the bound.
A program may use at most 128 MiB of HBM per device.

```python
import jax
import jax.numpy as jnp
from jax import lax

C = 256
HEADS = 8
MLP = 1024
GRID = 64
PIX = 512
DB = 16
LAYERS = 2
FRAMES = 8
SECTORS = 2


def draw_w_qkv(key, part):
    first = jax.random.fold_in(jax.random.fold_in(key, 11), 0)
    base = jnp.clip(jax.random.normal(first, (LAYERS, C, 3 * C), jnp.float32), -6.0, 6.0) * C ** (-0.5)
    return base.astype(jnp.bfloat16)


def touch_ends(result, own_key, least, top_value):
    dims = result.shape
    index_at = [jax.random.randint(jax.random.fold_in(own_key, axis), (), 0, dims[axis]) for axis in range(len(dims))]
    result = result.at[tuple(index_at)].set(least)
    longest = dims.index(max(dims))
    index_at[longest] = (index_at[longest] + 1) % dims[longest]
    return result.at[tuple(index_at)].set(top_value)


def block_levels(key, dims, cuts, least, high):
    factor_of, own = 1.0, jax.random.fold_in(key, 6)
    for dim, shards_of in cuts:
        steps = jnp.exp(jax.random.uniform(jax.random.fold_in(own, dim), (shards_of,), jnp.float32, least / len(cuts), high / len(cuts)))
        factor_of = factor_of * jnp.repeat(steps, dims[dim] // shards_of).reshape([-1 if axis == dim else 1 for axis in range(len(dims))])
    return factor_of


def normal_values(rng, extent, spread, most, shards=(), kind=jnp.bfloat16):
    factor_of = block_levels(rng, extent, shards, -0.22, 0.18) if shards else 1.0
    values = jax.random.normal(rng, extent, jnp.float32) * spread * factor_of
    return jnp.minimum(jnp.maximum(values, -most), most).astype(kind)


def setup_inputs(seed: int = 0, part: int = 0) -> dict:
    key_list = jax.random.split(jax.random.key(seed), 11)
    part_splits = jax.random.split(jax.random.fold_in(key_list[10], part), 11)
    return {
        "context": normal_values(part_splits[0], (FRAMES, SECTORS, PIX, C), 1.0, 6.0, ((0, 8), (1, 2))),
        "depth_weight": jnp.clip(1.0 * jax.random.uniform(part_splits[1], (FRAMES, SECTORS, DB, PIX), jnp.float32) ** block_levels(part_splits[1], (FRAMES, SECTORS, DB, PIX), ((0, 8), (1, 2)), -0.2, 0.2), 0.0, 1.0),
        "cell_ids": touch_ends(jax.random.randint(key_list[2], (SECTORS, DB, PIX), 0, GRID * GRID), jax.random.fold_in(key_list[2], 1), 0, (GRID * GRID) - 1).astype(jnp.int32),
        "time_embed": normal_values(key_list[3], (FRAMES, C), 0.5, 3.0),
        "norm_gain": jnp.clip(1.0 + 0.18 * jax.random.normal(key_list[4], (LAYERS, 2, C), jnp.float32), 0.1, 1.9),
        "w_qkv": draw_w_qkv(jax.random.fold_in(key_list[10], 71), part),
        "w_out": normal_values(key_list[6], (LAYERS, C, C), C ** -0.5, 0.375),
        "w_up": normal_values(key_list[7], (LAYERS, C, MLP), C ** -0.5, 0.375),
        "w_down": normal_values(key_list[8], (LAYERS, MLP, C), MLP ** -0.5, 0.1875),
        "conv_weight": normal_values(key_list[9], (3, 3, C, C), (9 * C) ** -0.5, 0.125),
    }


def pool_frame(context_frame, weight_frame, cell_ids):
    cell_count = GRID * GRID
    block_cells = min(512, cell_count)

    def one_sector(sector_inputs):
        features, weights, cell_index = sector_inputs

        def one_block(first_cell):
            target = first_cell + lax.broadcasted_iota(jnp.int32, (block_cells, 1), 0)
            matches = cell_index[:, None, :] == target[None]
            matrix = lax.optimization_barrier(jnp.sum(jnp.where(matches, weights[:, None, :], jnp.zeros_like(weights[:, None, :])), axis=0)).astype(jnp.bfloat16)
            return jnp.dot(matrix, features, preferred_element_type=jnp.float32).astype(jnp.bfloat16)
        starts = (jnp.arange(cell_count // block_cells) * block_cells).astype(jnp.int32)
        return lax.map(one_block, starts).reshape(cell_count, features.shape[-1])
    partials = lax.map(one_sector, (context_frame, weight_frame, cell_ids))
    return lax.optimization_barrier(jnp.sum(partials.astype(jnp.float32), axis=0)).astype(jnp.bfloat16)

def normalize(values, gain):
    return values * lax.rsqrt(lax.optimization_barrier(jnp.mean(values * values, axis=-1, keepdims=True)) + 1e-05) * gain

def encode_stack(tokens, time_embed, norm_gain, w_qkv, w_out, w_up, w_down):
    frame_count, cell_count, channels = tokens.shape
    head_size = channels // HEADS
    query_frame = lax.broadcasted_iota(jnp.int32, (frame_count, frame_count), 0)
    key_frame = lax.broadcasted_iota(jnp.int32, (frame_count, frame_count), 1)
    allowed = key_frame <= query_frame
    stream = (tokens.astype(jnp.float32) + time_embed[:, None, :].astype(jnp.float32)).reshape(frame_count * cell_count, channels)
    for number in range(LAYERS):
        normed = normalize(stream, norm_gain[number, 0]).astype(jnp.bfloat16)
        projected = jnp.dot(normed, w_qkv[number], preferred_element_type=jnp.float32).astype(jnp.bfloat16)
        projected = projected.reshape(frame_count, cell_count, 3, HEADS, head_size).astype(jnp.float32)
        scores = jnp.einsum('fchd,gchd->chfg', projected[:, :, 0], projected[:, :, 1]) * head_size ** (-0.5)
        scores = jnp.where(allowed, scores, -1e+30)
        largest = lax.optimization_barrier(jnp.max(scores, axis=-1, keepdims=True))
        raised = jnp.exp(scores - largest)
        soft_weights = (raised / lax.optimization_barrier(jnp.sum(raised, axis=-1, keepdims=True))).astype(jnp.bfloat16)
        mixed = jnp.einsum('chfg,gchd->fchd', soft_weights.astype(jnp.float32), projected[:, :, 2]).astype(jnp.bfloat16)
        mixed = mixed.reshape(frame_count * cell_count, channels)
        stream = stream + jnp.dot(mixed, w_out[number], preferred_element_type=jnp.float32)
        normed_second = normalize(stream, norm_gain[number, 1]).astype(jnp.bfloat16)
        hidden_units = jax.nn.gelu(jnp.dot(normed_second, w_up[number], preferred_element_type=jnp.float32), approximate=True).astype(jnp.bfloat16)
        stream = stream + jnp.dot(hidden_units, w_down[number], preferred_element_type=jnp.float32)
    return stream.reshape(frame_count, cell_count, channels).astype(jnp.bfloat16)

def convolve(frame_grid, conv_weight):
    padded = jnp.pad(frame_grid, ((1, 1), (1, 1), (0, 0)))
    summed = frame_grid.astype(jnp.float32)
    for offset in range(3):
        row_strip = padded[offset:offset + GRID]
        stacked = jnp.concatenate([row_strip[:, column:column + GRID] for column in range(3)], axis=-1)
        product = jnp.dot(stacked.reshape(GRID * GRID, 3 * C), conv_weight[offset].reshape(3 * C, C), preferred_element_type=jnp.float32)
        summed = summed + product.reshape(GRID, GRID, C)
    return summed.astype(jnp.bfloat16)

def reference(context, depth_weight, cell_ids, time_embed, norm_gain, w_qkv, w_out, w_up, w_down, conv_weight):

    def pool_one(frame_inputs):
        return pool_frame(frame_inputs[0], frame_inputs[1], cell_ids)
    pooled = lax.map(pool_one, (context, depth_weight))
    cell_count = GRID * GRID
    block_cells = min(256, cell_count)
    grouped = pooled.reshape(FRAMES, cell_count // block_cells, block_cells, C).transpose(1, 0, 2, 3)

    def encode_one(cell_group):
        return encode_stack(cell_group, time_embed, norm_gain, w_qkv, w_out, w_up, w_down)
    encoded = lax.map(encode_one, grouped)
    encoded = encoded.transpose(1, 0, 2, 3).reshape(FRAMES, GRID, GRID, C)

    def convolve_one(frame_grid):
        return convolve(frame_grid, conv_weight)
    return lax.map(convolve_one, encoded)
```

```python
import functools
import math

import jax
import jax.numpy as jnp
from jax import lax
from jax.experimental import pallas as pl
from jax.experimental.pallas import tpu as pltpu
from jax.sharding import PartitionSpec as P

HEADS = 8
GRID = 64
BF = jnp.bfloat16
F32 = jnp.float32
LANES16 = 16


def padded_2(cells, sides, width):
    for axis, dim in sides:
        count = lax.axis_size(axis)
        ends = count - 1
        head = lax.slice_in_dim(cells, 0, width, axis=dim)
        tail = lax.slice_in_dim(cells, cells.shape[dim] - width, cells.shape[dim], axis=dim)
        cells = jnp.concatenate(
            [
                lax.ppermute(tail, axis, [(i, (i + 1) % count) for i in range(ends)]),
                cells,
                lax.ppermute(head, axis, [((i + 1) % count, i) for i in range(ends)]),
            ],
            axis=dim,
        )
    return cells


def spread_rows(rows, out_ref):
    for d in range(rows.shape[0]):
        row = jnp.broadcast_to(rows[d : d + 1], (LANES16, rows.shape[1]))
        out_ref[d] = row.astype(BF)


def combine_bins(ids, weights, out_ref):
    rows = []
    for d in range(ids.shape[0]):
        same = jnp.where(ids == ids[d : d + 1], weights, 0.0)
        rows.append(jnp.sum(same, axis=0, keepdims=True))
    spread_rows(jnp.concatenate(rows, axis=0), out_ref)


def pool_block(ids, wide_ref, features, base, rows, loc_ref, matrix_ref):
    bins, pixels = ids.shape
    local = ids - base
    local = jnp.where((local >= 0) & (local < rows), local, -1).astype(F32)
    spread_rows(local, loc_ref)
    sub = min(64, rows)
    first = lax.broadcasted_iota(jnp.int32, (sub, pixels), 0).astype(F32)
    for part in range(rows // sub):
        cell = (first + float(part * sub)).astype(BF).reshape(sub // LANES16, LANES16, pixels)
        block = jnp.zeros(cell.shape, BF)
        for d in range(bins):
            block = jnp.where(cell == loc_ref[d][None], wide_ref[d][None], block)
        matrix_ref[part * sub : (part + 1) * sub] = block.reshape(sub, pixels)
    return jnp.dot(matrix_ref[...], features, preferred_element_type=F32).astype(BF)


def pool_kernel(rows, ids_ref, weight_ref, context_ref, out_ref, wide_ref, loc_ref, matrix_ref):
    sectors = ids_ref.shape[0]
    start = lax.axis_index("sector") * out_ref.shape[0]

    for s in range(sectors):
        combine_bins(ids_ref[s], weight_ref[s], wide_ref.at[s])

    @pl.loop(0, out_ref.shape[0] // rows)
    def _(step):
        total = None
        for s in range(sectors):
            part = pool_block(
                ids_ref[s],
                wide_ref.at[s],
                context_ref[s],
                start + step * rows,
                rows,
                loc_ref,
                matrix_ref,
            ).astype(F32)
            total = part if total is None else total + part
        out_ref[pl.ds(pl.multiple_of(step * rows, rows), rows)] = total.astype(BF)


def normalize(values, gain):
    return values * lax.rsqrt(jnp.mean(values * values, axis=-1, keepdims=True) + 1e-05) * gain


def encode_chunk(tokens, time_ref, gain_ref, qkv_ref, out_w_ref, up_ref, down_ref, head_sum, scratch):
    stream_ref, q_ref, k_ref, v_ref, mixed_ref = scratch
    frames, cells, channels = tokens.shape
    scale = (channels // HEADS) ** (-0.5) * math.log2(math.e)
    stream_ref[...] = tokens.astype(F32) + time_ref[...].astype(F32)[:, None, :]
    flat = (frames * cells, channels)

    def attend(f, count, masked):
        query = q_ref[f]
        product = (k_ref[0:count] * query[None]).reshape(count * cells, channels)
        high = product.astype(BF)
        low = (product - high.astype(F32)).astype(BF)
        scores = jnp.dot(high, head_sum, preferred_element_type=F32)
        scores = scores + jnp.dot(low, head_sum, preferred_element_type=F32)
        scores = scores.reshape(count, cells, channels)
        if masked:
            frame = lax.broadcasted_iota(jnp.int32, scores.shape, 0)
            scores = jnp.where(frame <= f, scores, -1e30)
        raised = jnp.exp2(scores - jnp.max(scores, axis=0, keepdims=True))
        mixed = jnp.sum(raised * v_ref[0:count], axis=0) / jnp.sum(raised, axis=0)
        mixed_ref[f] = mixed.astype(BF)

    def layer(l, carry):
        stream = stream_ref[...].reshape(flat)
        normed = normalize(stream, gain_ref[l, 0:1]).astype(BF)
        for i, ref in enumerate((q_ref, k_ref, v_ref)):
            part = jnp.dot(
                normed,
                qkv_ref[l, :, i * channels : (i + 1) * channels],
                preferred_element_type=F32,
            )
            part = part.astype(BF).astype(F32)
            ref[...] = (part * scale if i == 0 else part).reshape(ref.shape)
        if frames <= 8:
            for f in range(frames):
                attend(f, f + 1, False)
        else:
            lax.fori_loop(0, frames, lambda f, c: (attend(f, frames, True), c)[1], 0)
        stream = stream_ref[...].reshape(flat) + jnp.dot(
            mixed_ref[...].reshape(flat), out_w_ref[l], preferred_element_type=F32
        )
        normed = normalize(stream, gain_ref[l, 1:2]).astype(BF)
        hidden_width = up_ref.shape[2]
        step = min(256, hidden_width)
        for j in range(0, hidden_width, step):
            hidden = jnp.dot(normed, up_ref[l, :, j : j + step], preferred_element_type=F32)
            hidden = jax.nn.gelu(hidden, approximate=True).astype(BF)
            stream = stream + jnp.dot(
                hidden, down_ref[l, j : j + step, :], preferred_element_type=F32
            )
        stream_ref[...] = stream.reshape(stream_ref.shape)
        return carry

    lax.fori_loop(0, qkv_ref.shape[0], layer, 0)
    return stream_ref[...].astype(BF)


def head_matrix(channels):
    size = channels // HEADS
    row = lax.broadcasted_iota(jnp.int32, (channels, channels), 0) // size
    column = lax.broadcasted_iota(jnp.int32, (channels, channels), 1) // size
    return (row == column).astype(F32).astype(BF)


def encode_scratch(frames, cells, channels):
    shape = (frames, cells, channels)
    return [pltpu.VMEM(shape, F32)] * 4 + [pltpu.VMEM(shape, BF)]


def encode_kernel(tok_ref, time_ref, gain_ref, qkv_ref, ow_ref, up_ref, down_ref, out_ref, *scratch):
    channels = tok_ref.shape[-1]
    out_ref[...] = encode_chunk(
        tok_ref[...],
        time_ref,
        gain_ref,
        qkv_ref,
        ow_ref,
        up_ref,
        down_ref,
        head_matrix(channels),
        scratch,
    )


def body(
    context, depth_weight, cell_ids, time_embed, norm_gain, w_qkv, w_out, w_up, w_down, conv_weight
):
    tm_count = lax.axis_size("tm")
    frames_dev, _, pixels, channels = context.shape
    bins = cell_ids.shape[1]
    sectors = lax.axis_size("sector")
    band_cells = GRID * GRID // sectors
    piece_cells = band_cells // tm_count
    ids = lax.all_gather(cell_ids[0], "sector")
    weights = lax.all_gather(depth_weight[0, 0], "sector")
    features = lax.all_gather(context[0, 0], "sector")
    rows = min(256, band_cells)
    vmem = pl.BlockSpec(memory_space=pltpu.VMEM)
    pooled = pl.pallas_call(
        functools.partial(pool_kernel, rows),
        out_shape=jax.ShapeDtypeStruct((band_cells, channels), BF),
        in_specs=[vmem] * 3,
        out_specs=vmem,
        scratch_shapes=[
            pltpu.VMEM((sectors, bins, LANES16, pixels), BF),
            pltpu.VMEM((bins, LANES16, pixels), BF),
            pltpu.VMEM((rows, pixels), BF),
        ],
        compiler_params=pltpu.CompilerParams(vmem_limit_bytes=48 * 2**20),
    )(ids, weights, features)
    sectioned = pooled.reshape(frames_dev, tm_count, piece_cells, channels)
    received = lax.all_to_all(sectioned, "tm", split_axis=1, concat_axis=0, tiled=True)
    tokens = received.reshape(tm_count, piece_cells, channels)
    frames = tm_count
    chunk = math.gcd(64, piece_cells)
    block = pl.BlockSpec((frames, chunk, channels), lambda i: (0, i, 0))
    encoded = pl.pallas_call(
        encode_kernel,
        grid=(piece_cells // chunk,),
        out_shape=jax.ShapeDtypeStruct(tokens.shape, BF),
        in_specs=[block] + [vmem] * 6,
        out_specs=block,
        scratch_shapes=encode_scratch(frames, chunk, channels),
        compiler_params=pltpu.CompilerParams(vmem_limit_bytes=56 * 2**20),
    )(tokens, time_embed, norm_gain, w_qkv, w_out, w_up, w_down)
    returned = lax.all_to_all(encoded, "tm", split_axis=0, concat_axis=1, tiled=True)
    row_count = band_cells // GRID
    encoded = returned.reshape(frames_dev, row_count, GRID, channels)
    padded = padded_2(encoded, (("sector", 1),), 1)
    padded = jnp.pad(padded, ((0, 0), (0, 0), (1, 1), (0, 0)))
    summed = encoded.astype(jnp.float32)
    for offset in range(3):
        row_strip = padded[:, offset : offset + row_count]
        stacked = jnp.concatenate(
            [row_strip[:, :, column : column + GRID] for column in range(3)], axis=-1
        )
        product = jnp.dot(
            stacked.reshape(frames_dev * row_count * GRID, 3 * channels),
            conv_weight[offset].reshape(3 * channels, channels),
            preferred_element_type=jnp.float32,
        )
        summed = summed + product.reshape(summed.shape)
    return summed.astype(jnp.bfloat16)


def solution(mesh):
    return jax.shard_map(
        body,
        mesh=mesh,
        in_specs=(
            P(("groups", "tm"), "sector", None, None),
            P(("groups", "tm"), "sector", None, None),
            P("sector", None, None),
            P(),
            P(),
            P(),
            P(),
            P(),
            P(),
            P(),
        ),
        out_specs=P(("groups", "tm"), "sector", None, None),
        check_vma=False,
    )
```

```python
import functools
import math

import jax
import jax.numpy as jnp
from jax import lax
from jax.experimental import pallas as pl
from jax.experimental.pallas import tpu as pltpu
from jax.sharding import PartitionSpec as P

HEADS = 8
GRID = 64
BF = jnp.bfloat16
F32 = jnp.float32
LANES16 = 16


def spread_rows(rows, out_ref):
    for d in range(rows.shape[0]):
        row = jnp.broadcast_to(rows[d : d + 1], (LANES16, rows.shape[1]))
        out_ref[d] = row.astype(BF)


def combine_bins(ids, weights, out_ref):
    rows = []
    for d in range(ids.shape[0]):
        same = jnp.where(ids == ids[d : d + 1], weights, 0.0)
        rows.append(jnp.sum(same, axis=0, keepdims=True))
    spread_rows(jnp.concatenate(rows, axis=0), out_ref)


def pool_block(ids, wide_ref, features, base, rows, loc_ref, matrix_ref):
    bins, pixels = ids.shape
    local = ids - base
    local = jnp.where((local >= 0) & (local < rows), local, -1).astype(F32)
    spread_rows(local, loc_ref)
    sub = min(64, rows)
    first = lax.broadcasted_iota(jnp.int32, (sub, pixels), 0).astype(F32)
    for part in range(rows // sub):
        cell = (first + float(part * sub)).astype(BF).reshape(sub // LANES16, LANES16, pixels)
        block = jnp.zeros(cell.shape, BF)
        for d in range(bins):
            block = jnp.where(cell == loc_ref[d][None], wide_ref[d][None], block)
        matrix_ref[part * sub : (part + 1) * sub] = block.reshape(sub, pixels)
    return jnp.dot(matrix_ref[...], features, preferred_element_type=F32).astype(BF)


def normalize(values, gain):
    return values * lax.rsqrt(jnp.mean(values * values, axis=-1, keepdims=True) + 1e-05) * gain


def encode_chunk(tokens, time_ref, gain_ref, qkv_ref, out_w_ref, up_ref, down_ref, head_sum, scratch):
    stream_ref, q_ref, k_ref, v_ref, mixed_ref = scratch
    frames, cells, channels = tokens.shape
    scale = (channels // HEADS) ** (-0.5) * math.log2(math.e)
    stream_ref[...] = tokens.astype(F32) + time_ref[...].astype(F32)[:, None, :]
    flat = (frames * cells, channels)

    def attend(f, count, masked):
        query = q_ref[f]
        product = (k_ref[0:count] * query[None]).reshape(count * cells, channels)
        high = product.astype(BF)
        low = (product - high.astype(F32)).astype(BF)
        scores = jnp.dot(high, head_sum, preferred_element_type=F32)
        scores = scores + jnp.dot(low, head_sum, preferred_element_type=F32)
        scores = scores.reshape(count, cells, channels)
        if masked:
            frame = lax.broadcasted_iota(jnp.int32, scores.shape, 0)
            scores = jnp.where(frame <= f, scores, -1e30)
        raised = jnp.exp2(scores - jnp.max(scores, axis=0, keepdims=True))
        mixed = jnp.sum(raised * v_ref[0:count], axis=0) / jnp.sum(raised, axis=0)
        mixed_ref[f] = mixed.astype(BF)

    def layer(l, carry):
        stream = stream_ref[...].reshape(flat)
        normed = normalize(stream, gain_ref[l, 0:1]).astype(BF)
        for i, ref in enumerate((q_ref, k_ref, v_ref)):
            part = jnp.dot(
                normed,
                qkv_ref[l, :, i * channels : (i + 1) * channels],
                preferred_element_type=F32,
            )
            part = part.astype(BF).astype(F32)
            ref[...] = (part * scale if i == 0 else part).reshape(ref.shape)
        if frames <= 8:
            for f in range(frames):
                attend(f, f + 1, False)
        else:
            lax.fori_loop(0, frames, lambda f, c: (attend(f, frames, True), c)[1], 0)
        stream = stream_ref[...].reshape(flat) + jnp.dot(
            mixed_ref[...].reshape(flat), out_w_ref[l], preferred_element_type=F32
        )
        normed = normalize(stream, gain_ref[l, 1:2]).astype(BF)
        hidden_width = up_ref.shape[2]
        step = min(256, hidden_width)
        for j in range(0, hidden_width, step):
            hidden = jnp.dot(normed, up_ref[l, :, j : j + step], preferred_element_type=F32)
            hidden = jax.nn.gelu(hidden, approximate=True).astype(BF)
            stream = stream + jnp.dot(
                hidden, down_ref[l, j : j + step, :], preferred_element_type=F32
            )
        stream_ref[...] = stream.reshape(stream_ref.shape)
        return carry

    lax.fori_loop(0, qkv_ref.shape[0], layer, 0)
    return stream_ref[...].astype(BF)


def head_matrix(channels):
    size = channels // HEADS
    row = lax.broadcasted_iota(jnp.int32, (channels, channels), 0) // size
    column = lax.broadcasted_iota(jnp.int32, (channels, channels), 1) // size
    return (row == column).astype(F32).astype(BF)


def encode_scratch(frames, cells, channels):
    shape = (frames, cells, channels)
    return [pltpu.VMEM(shape, F32)] * 4 + [pltpu.VMEM(shape, BF)]


def conv_rows(x_ref, cat_ref, first, count):
    channels = x_ref.shape[1]
    centre = x_ref[pl.ds(first, count)]
    values = centre.astype(F32)
    column = lax.broadcasted_iota(jnp.int32, values.shape, 0) % GRID
    left = jnp.where(column == 0, 0.0, pltpu.roll(values, 1, 0)).astype(BF)
    right = jnp.where(column == GRID - 1, 0.0, pltpu.roll(values, count - 1, 0)).astype(BF)
    cat_ref[pl.ds(first, count), 0:channels] = left
    cat_ref[pl.ds(first, count), channels : 2 * channels] = centre
    cat_ref[pl.ds(first, count), 2 * channels :] = right


def fused_kernel(
    tm_count,
    sectors,
    piece,
    chunk,
    context_ref,
    weight_ref,
    ids_ref,
    time_ref,
    gain_ref,
    qkv_hbm,
    ow_hbm,
    up_hbm,
    down_hbm,
    conv_hbm,
    result_ref,
    qkv_ref,
    ow_ref,
    up_ref,
    down_ref,
    conv_ref,
    far_context,
    far_weight,
    far_ids,
    wide_ref,
    perm_ref,
    loc_ref,
    matrix_ref,
    send_ref,
    recv_ref,
    enc_ref,
    x_ref,
    cat_ref,
    load_sem,
    sector_send,
    sector_recv,
    go_send,
    go_recv,
    back_send,
    back_recv,
    edge_send,
    edge_recv,
    *scratch,
):
    me = lax.axis_index("tm")
    sector = lax.axis_index("sector")
    pixels, channels = context_ref.shape
    chunks = piece // chunk
    band = tm_count * piece
    bins = ids_ref.shape[0]

    loads = []
    for i, (a, b) in enumerate(
        (
            (qkv_hbm, qkv_ref),
            (ow_hbm, ow_ref),
            (up_hbm, up_ref),
            (down_hbm, down_ref),
            (conv_hbm, conv_ref),
        )
    ):
        loads.append(pltpu.make_async_copy(a, b, load_sem.at[i]))
        loads[-1].start()

    barrier = pltpu.get_barrier_semaphore()

    @pl.loop(1, tm_count)
    def _(o):
        pl.semaphore_signal(
            barrier,
            inc=1,
            device_id={"tm": lax.rem(me + o, tm_count)},
            device_id_type=pl.DeviceIdType.MESH,
        )

    for o in range(1, sectors):
        pl.semaphore_signal(
            barrier,
            inc=1,
            device_id={"sector": lax.rem(sector + o, sectors)},
            device_id_type=pl.DeviceIdType.MESH,
        )
    pl.semaphore_wait(barrier, tm_count - 1 + sectors - 1)

    swaps = []
    for o in range(1, sectors):
        for i, (a, b) in enumerate(
            ((ids_ref, far_ids), (weight_ref, far_weight), (context_ref, far_context))
        ):
            swaps.append(
                pltpu.make_async_remote_copy(
                    src_ref=a,
                    dst_ref=b.at[o - 1],
                    send_sem=sector_send.at[o - 1, i],
                    recv_sem=sector_recv.at[o - 1, i],
                    device_id={"sector": lax.rem(sector + o, sectors)},
                    device_id_type=pl.DeviceIdType.MESH,
                )
            )
            swaps[-1].start()

    def prepare(s, ids, weights):
        combine_bins(ids, weights, wide_ref.at[s])
        local = ids - sector * band
        inside = (local >= 0) & (local < band)
        local = jnp.where(inside, local, 0)
        owner, rest = local // piece, local % piece
        place = ((rest // chunk) * tm_count + owner) * chunk + rest % chunk
        perm_ref[s] = jnp.where(inside, place, -1)

    prepare(0, ids_ref[...], weight_ref[...])
    for o in range(1, sectors):
        for copy in swaps[3 * (o - 1) : 3 * o]:
            copy.wait()
        prepare(o, far_ids[o - 1], far_weight[o - 1])

    rows = matrix_ref.shape[0]
    blocks = tm_count * chunk // rows
    per = rows // chunk

    def go_copy(c, target, source):
        return pltpu.make_async_remote_copy(
            src_ref=send_ref.at[c * tm_count + target],
            dst_ref=recv_ref.at[c, source],
            send_sem=go_send.at[c, target],
            recv_sem=go_recv.at[c, source],
            device_id={"tm": target},
            device_id_type=pl.DeviceIdType.MESH,
        )

    def back_copy(c, target, source):
        return pltpu.make_async_remote_copy(
            src_ref=enc_ref.at[c, target],
            dst_ref=x_ref.at[pl.ds(pl.multiple_of(GRID + source * piece + c * chunk, 16), chunk)],
            send_sem=back_send.at[c, target],
            recv_sem=back_recv.at[c, source],
            device_id={"tm": target},
            device_id_type=pl.DeviceIdType.MESH,
        )

    @pl.loop(0, chunks)
    def _(c):
        @pl.loop(0, blocks)
        def _(b):
            step = c * blocks + b
            total = None
            for s in range(sectors):
                features = context_ref[...] if s == 0 else far_context[s - 1]
                part = pool_block(
                    perm_ref[s], wide_ref.at[s], features, step * rows, rows, loc_ref, matrix_ref
                ).astype(F32)
                total = part if total is None else total + part
            send_ref[pl.ds(step * per, per)] = total.astype(BF).reshape(per, chunk, channels)

        @pl.loop(1, tm_count)
        def _(o):
            go_copy(c, lax.rem(me + o, tm_count), me).start()

        recv_ref[c, me] = send_ref[c * tm_count + me]

    for load in loads:
        load.wait()
    head_sum = head_matrix(channels)

    @pl.loop(0, chunks)
    def _(c):
        @pl.loop(1, tm_count)
        def _(o):
            go_copy(c, me, lax.rem(me + tm_count - o, tm_count)).wait_recv()

        enc_ref[c] = encode_chunk(
            recv_ref[c],
            time_ref,
            gain_ref,
            qkv_ref,
            ow_ref,
            up_ref,
            down_ref,
            head_sum,
            scratch,
        )

        @pl.loop(1, tm_count)
        def _(o):
            back_copy(c, lax.rem(me + o, tm_count), me).start()

        here = pl.multiple_of(GRID + me * piece + c * chunk, 16)
        x_ref[pl.ds(here, chunk)] = enc_ref[c, me]

    @pl.loop(0, chunks)
    def _(c):
        @pl.loop(1, tm_count)
        def _(o):
            back_copy(c, me, lax.rem(me + tm_count - o, tm_count)).wait_recv()

    def edge_copy(way):
        return pltpu.make_async_remote_copy(
            src_ref=x_ref.at[pl.ds(band if way == 0 else GRID, GRID)],
            dst_ref=x_ref.at[pl.ds(0 if way == 0 else band + GRID, GRID)],
            send_sem=edge_send.at[way],
            recv_sem=edge_recv.at[way],
            device_id={"sector": lax.rem(sector + (1 if way == 0 else sectors - 1), sectors)},
            device_id_type=pl.DeviceIdType.MESH,
        )

    blank = jnp.zeros((GRID, channels), BF)

    @pl.when(sector < sectors - 1)
    def _():
        edge_copy(0).start()

    @pl.when(sector > 0)
    def _():
        edge_copy(1).start()

    @pl.when(sector == 0)
    def _():
        x_ref[0:GRID] = blank

    @pl.when(sector == sectors - 1)
    def _():
        x_ref[band + GRID : band + 2 * GRID] = blank

    tall = math.gcd(band, 8 * GRID)

    @pl.loop(0, band // tall)
    def _(i):
        conv_rows(x_ref, cat_ref, pl.multiple_of(GRID + i * tall, GRID), tall)

    @pl.when(sector > 0)
    def _():
        edge_copy(0).wait_recv()

    @pl.when(sector < sectors - 1)
    def _():
        edge_copy(1).wait_recv()

    conv_rows(x_ref, cat_ref, 0, GRID)
    conv_rows(x_ref, cat_ref, band + GRID, GRID)

    @pl.loop(0, band // tall)
    def _(i):
        first = pl.multiple_of(i * tall, GRID)
        total = x_ref[pl.ds(pl.multiple_of(first + GRID, GRID), tall)].astype(F32)
        for r in range(3):
            strip = cat_ref[pl.ds(pl.multiple_of(first + r * GRID, GRID), tall)]
            total = total + jnp.dot(strip, conv_ref[r], preferred_element_type=F32)
        result_ref[pl.ds(first, tall)] = total.astype(BF)

    @pl.when(sector < sectors - 1)
    def _():
        edge_copy(0).wait_send()

    @pl.when(sector > 0)
    def _():
        edge_copy(1).wait_send()

    @pl.loop(0, chunks)
    def _(c):
        @pl.loop(1, tm_count)
        def _(o):
            target = lax.rem(me + o, tm_count)
            go_copy(c, target, me).wait_send()
            back_copy(c, target, me).wait_send()


def body(
    context, depth_weight, cell_ids, time_embed, norm_gain, w_qkv, w_out, w_up, w_down, conv_weight
):
    tm_count = lax.axis_size("tm")
    sectors = lax.axis_size("sector")
    pixels, channels = context.shape[2:]
    bins = cell_ids.shape[1]
    band = GRID * GRID // sectors
    piece = band // tm_count
    chunk = math.gcd(64, piece)
    chunks = piece // chunk
    rows = math.gcd(256, tm_count * chunk)
    conv_flat = conv_weight.reshape(3, 3 * channels, channels)
    vmem = pl.BlockSpec(memory_space=pltpu.VMEM)
    anywhere = pl.BlockSpec(memory_space=pl.ANY)
    dma = pltpu.SemaphoreType.DMA
    far = sectors - 1
    result = pl.pallas_call(
        functools.partial(fused_kernel, tm_count, sectors, piece, chunk),
        out_shape=jax.ShapeDtypeStruct((band, channels), BF),
        in_specs=[vmem] * 5 + [anywhere] * 5,
        out_specs=vmem,
        scratch_shapes=[
            pltpu.VMEM(w_qkv.shape, BF),
            pltpu.VMEM(w_out.shape, BF),
            pltpu.VMEM(w_up.shape, BF),
            pltpu.VMEM(w_down.shape, BF),
            pltpu.VMEM(conv_flat.shape, BF),
            pltpu.VMEM((far, pixels, channels), BF),
            pltpu.VMEM((far, bins, pixels), F32),
            pltpu.VMEM((far, bins, pixels), jnp.int32),
            pltpu.VMEM((sectors, bins, LANES16, pixels), BF),
            pltpu.VMEM((sectors, bins, pixels), jnp.int32),
            pltpu.VMEM((bins, LANES16, pixels), BF),
            pltpu.VMEM((rows, pixels), BF),
            pltpu.VMEM((chunks * tm_count, chunk, channels), BF),
            pltpu.VMEM((chunks, tm_count, chunk, channels), BF),
            pltpu.VMEM((chunks, tm_count, chunk, channels), BF),
            pltpu.VMEM((band + 2 * GRID, channels), BF),
            pltpu.VMEM((band + 2 * GRID, 3 * channels), BF),
            dma((5,)),
            dma((far, 3)),
            dma((far, 3)),
            dma((chunks, tm_count)),
            dma((chunks, tm_count)),
            dma((chunks, tm_count)),
            dma((chunks, tm_count)),
            dma((2,)),
            dma((2,)),
        ]
        + encode_scratch(tm_count, chunk, channels),
        compiler_params=pltpu.CompilerParams(
            collective_id=0, has_side_effects=True, vmem_limit_bytes=60 * 2**20
        ),
    )(
        context[0, 0],
        depth_weight[0, 0],
        cell_ids[0],
        time_embed,
        norm_gain,
        w_qkv,
        w_out,
        w_up,
        w_down,
        conv_flat,
    )
    return result.reshape(1, band // GRID, GRID, channels)


def solution(mesh):
    return jax.shard_map(
        body,
        mesh=mesh,
        in_specs=(
            P(("groups", "tm"), "sector", None, None),
            P(("groups", "tm"), "sector", None, None),
            P("sector", None, None),
            P(),
            P(),
            P(),
            P(),
            P(),
            P(),
            P(),
        ),
        out_specs=P(("groups", "tm"), "sector", None, None),
        check_vma=False,
    )
```

```python
import functools
import math

import jax
import jax.numpy as jnp
from jax import lax
from jax.experimental import pallas as pl
from jax.experimental.pallas import tpu as pltpu
from jax.sharding import PartitionSpec as P

HEADS = 8
GRID = 64
BF = jnp.bfloat16
F32 = jnp.float32
LANES16 = 16


def spread_rows(rows, out_ref):
    for d in range(rows.shape[0]):
        row = jnp.broadcast_to(rows[d : d + 1], (LANES16, rows.shape[1]))
        out_ref[d] = row.astype(BF)


def combine_bins(ids, weights, out_ref):
    rows = []
    for d in range(ids.shape[0]):
        same = jnp.where(ids == ids[d : d + 1], weights, 0.0)
        rows.append(jnp.sum(same, axis=0, keepdims=True))
    spread_rows(jnp.concatenate(rows, axis=0), out_ref)


def pool_block(ids, wide_ref, features, base, rows, loc_ref, matrix_ref):
    bins, pixels = ids.shape
    local = ids - base
    local = jnp.where((local >= 0) & (local < rows), local, -1).astype(F32)
    spread_rows(local, loc_ref)
    sub = min(64, rows)
    first = lax.broadcasted_iota(jnp.int32, (sub, pixels), 0).astype(F32)
    for part in range(rows // sub):
        cell = (first + float(part * sub)).astype(BF).reshape(sub // LANES16, LANES16, pixels)
        block = jnp.zeros(cell.shape, BF)
        for d in range(bins):
            block = jnp.where(cell == loc_ref[d][None], wide_ref[d][None], block)
        matrix_ref[part * sub : (part + 1) * sub] = block.reshape(sub, pixels)
    return jnp.dot(matrix_ref[...], features, preferred_element_type=F32).astype(BF)


def normalize(values, gain):
    return values * lax.rsqrt(jnp.mean(values * values, axis=-1, keepdims=True) + 1e-05) * gain


def encode_chunk(tokens, time_ref, gain_ref, qkv_ref, out_w_ref, up_ref, down_ref, head_sum, scratch):
    stream_ref, q_ref, k_ref, v_ref, mixed_ref = scratch
    frames, cells, channels = tokens.shape
    scale = (channels // HEADS) ** (-0.5) * math.log2(math.e)
    stream_ref[...] = tokens.astype(F32) + time_ref[...].astype(F32)[:, None, :]
    flat = (frames * cells, channels)

    def attend(f, count, masked):
        query = q_ref[f]
        product = (k_ref[0:count] * query[None]).reshape(count * cells, channels)
        high = product.astype(BF)
        low = (product - high.astype(F32)).astype(BF)
        scores = jnp.dot(high, head_sum, preferred_element_type=F32)
        scores = scores + jnp.dot(low, head_sum, preferred_element_type=F32)
        scores = scores.reshape(count, cells, channels)
        if masked:
            frame = lax.broadcasted_iota(jnp.int32, scores.shape, 0)
            scores = jnp.where(frame <= f, scores, -1e30)
        raised = jnp.exp2(scores - jnp.max(scores, axis=0, keepdims=True))
        mixed = jnp.sum(raised * v_ref[0:count], axis=0) / jnp.sum(raised, axis=0)
        mixed_ref[f] = mixed.astype(BF)

    def layer(l, carry):
        stream = stream_ref[...].reshape(flat)
        normed = normalize(stream, gain_ref[l, 0:1]).astype(BF)
        for i, ref in enumerate((q_ref, k_ref, v_ref)):
            part = jnp.dot(
                normed,
                qkv_ref[l, :, i * channels : (i + 1) * channels],
                preferred_element_type=F32,
            )
            part = part.astype(BF).astype(F32)
            ref[...] = (part * scale if i == 0 else part).reshape(ref.shape)
        if frames <= 8:
            for f in range(frames):
                attend(f, f + 1, False)
        else:
            lax.fori_loop(0, frames, lambda f, c: (attend(f, frames, True), c)[1], 0)
        stream = stream_ref[...].reshape(flat) + jnp.dot(
            mixed_ref[...].reshape(flat), out_w_ref[l], preferred_element_type=F32
        )
        normed = normalize(stream, gain_ref[l, 1:2]).astype(BF)
        hidden_width = up_ref.shape[2]
        step = min(256, hidden_width)
        for j in range(0, hidden_width, step):
            hidden = jnp.dot(normed, up_ref[l, :, j : j + step], preferred_element_type=F32)
            hidden = jax.nn.gelu(hidden, approximate=True).astype(BF)
            stream = stream + jnp.dot(
                hidden, down_ref[l, j : j + step, :], preferred_element_type=F32
            )
        stream_ref[...] = stream.reshape(stream_ref.shape)
        return carry

    lax.fori_loop(0, qkv_ref.shape[0], layer, 0)
    return stream_ref[...].astype(BF)


def head_matrix(channels):
    size = channels // HEADS
    row = lax.broadcasted_iota(jnp.int32, (channels, channels), 0) // size
    column = lax.broadcasted_iota(jnp.int32, (channels, channels), 1) // size
    return (row == column).astype(F32).astype(BF)


def encode_scratch(frames, cells, channels):
    shape = (frames, cells, channels)
    return [pltpu.VMEM(shape, F32)] * 4 + [pltpu.VMEM(shape, BF)]


def widen_row(row, cat_ref, place):
    channels = row.shape[1]
    values = row.astype(F32)
    column = lax.broadcasted_iota(jnp.int32, values.shape, 0)
    left = jnp.where(column == 0, 0.0, pltpu.roll(values, 1, 0)).astype(BF)
    right = jnp.where(column == GRID - 1, 0.0, pltpu.roll(values, GRID - 1, 0)).astype(BF)
    cat_ref[place, :, 0:channels] = left
    cat_ref[place, :, channels : 2 * channels] = row
    cat_ref[place, :, 2 * channels :] = right


def fused_kernel(
    tm_count,
    sectors,
    piece,
    chunk,
    context_ref,
    weight_ref,
    ids_ref,
    time_ref,
    gain_ref,
    qkv_hbm,
    ow_hbm,
    up_hbm,
    down_hbm,
    conv_hbm,
    result_ref,
    qkv_ref,
    ow_ref,
    up_ref,
    down_ref,
    conv_ref,
    far_context,
    far_weight,
    far_ids,
    wide_ref,
    perm_ref,
    loc_ref,
    matrix_ref,
    send_ref,
    recv_ref,
    enc_ref,
    x_ref,
    cat_ref,
    sum_ref,
    load_sem,
    sector_send,
    sector_recv,
    go_send,
    go_recv,
    back_send,
    back_recv,
    edge_send,
    edge_recv,
    *scratch,
):
    me = lax.axis_index("tm")
    sector = lax.axis_index("sector")
    pixels, channels = context_ref.shape
    chunks = piece // chunk
    band = tm_count * piece
    bins = ids_ref.shape[0]

    loads = []
    for i, (a, b) in enumerate(
        (
            (qkv_hbm, qkv_ref),
            (ow_hbm, ow_ref),
            (up_hbm, up_ref),
            (down_hbm, down_ref),
            (conv_hbm, conv_ref),
        )
    ):
        loads.append(pltpu.make_async_copy(a, b, load_sem.at[i]))
        loads[-1].start()

    barrier = pltpu.get_barrier_semaphore()

    @pl.loop(1, tm_count)
    def _(o):
        pl.semaphore_signal(
            barrier,
            inc=1,
            device_id={"tm": lax.rem(me + o, tm_count)},
            device_id_type=pl.DeviceIdType.MESH,
        )

    for o in range(1, sectors):
        pl.semaphore_signal(
            barrier,
            inc=1,
            device_id={"sector": lax.rem(sector + o, sectors)},
            device_id_type=pl.DeviceIdType.MESH,
        )
    pl.semaphore_wait(barrier, tm_count - 1 + sectors - 1)

    swaps = []
    for o in range(1, sectors):
        for i, (a, b) in enumerate(
            ((ids_ref, far_ids), (weight_ref, far_weight), (context_ref, far_context))
        ):
            swaps.append(
                pltpu.make_async_remote_copy(
                    src_ref=a,
                    dst_ref=b.at[o - 1],
                    send_sem=sector_send.at[o - 1, i],
                    recv_sem=sector_recv.at[o - 1, i],
                    device_id={"sector": lax.rem(sector + o, sectors)},
                    device_id_type=pl.DeviceIdType.MESH,
                )
            )
            swaps[-1].start()

    def prepare(s, ids, weights):
        combine_bins(ids, weights, wide_ref.at[s])
        local = ids - sector * band
        inside = (local >= 0) & (local < band)
        local = jnp.where(inside, local, 0)
        owner, rest = local // piece, local % piece
        place = ((rest // chunk) * tm_count + owner) * chunk + rest % chunk
        perm_ref[s] = jnp.where(inside, place, -1)

    prepare(0, ids_ref[...], weight_ref[...])
    for o in range(1, sectors):
        for copy in swaps[3 * (o - 1) : 3 * o]:
            copy.wait()
        prepare(o, far_ids[o - 1], far_weight[o - 1])

    rows = matrix_ref.shape[0]
    blocks = tm_count * chunk // rows
    per = rows // chunk

    def go_copy(c, target, source):
        return pltpu.make_async_remote_copy(
            src_ref=send_ref.at[c * tm_count + target],
            dst_ref=recv_ref.at[c, source],
            send_sem=go_send.at[c, target],
            recv_sem=go_recv.at[c, source],
            device_id={"tm": target},
            device_id_type=pl.DeviceIdType.MESH,
        )

    def back_copy(c, target, source):
        return pltpu.make_async_remote_copy(
            src_ref=enc_ref.at[c, target],
            dst_ref=x_ref.at[1 + source * chunks + c],
            send_sem=back_send.at[c, target],
            recv_sem=back_recv.at[c, source],
            device_id={"tm": target},
            device_id_type=pl.DeviceIdType.MESH,
        )

    @pl.loop(0, chunks)
    def _(c):
        @pl.loop(0, blocks)
        def _(i):
            b = lax.rem(i + 1 + lax.div(me, per), blocks)
            step = c * blocks + b
            total = None
            for s in range(sectors):
                features = context_ref[...] if s == 0 else far_context[s - 1]
                part = pool_block(
                    perm_ref[s], wide_ref.at[s], features, step * rows, rows, loc_ref, matrix_ref
                ).astype(F32)
                total = part if total is None else total + part
            send_ref[pl.ds(step * per, per)] = total.astype(BF).reshape(per, chunk, channels)

            @pl.loop(b * per, b * per + per)
            def _(target):
                @pl.when(target != me)
                def _():
                    go_copy(c, target, me).start()

        recv_ref[c, me] = send_ref[c * tm_count + me]

    sum_ref[...] = jnp.zeros_like(sum_ref)
    for load in loads:
        load.wait()
    head_sum = head_matrix(channels)

    @pl.loop(0, chunks)
    def _(c):
        @pl.loop(1, tm_count)
        def _(o):
            go_copy(c, me, lax.rem(me + tm_count - o, tm_count)).wait_recv()

        enc_ref[c] = encode_chunk(
            recv_ref[c],
            time_ref,
            gain_ref,
            qkv_ref,
            ow_ref,
            up_ref,
            down_ref,
            head_sum,
            scratch,
        )

        @pl.loop(1, tm_count)
        def _(o):
            back_copy(c, lax.rem(me + o, tm_count), me).start()

        x_ref[1 + me * chunks + c] = enc_ref[c, me]

    height = tm_count * chunks

    def edge_copy(way):
        return pltpu.make_async_remote_copy(
            src_ref=x_ref.at[height if way == 0 else 1],
            dst_ref=x_ref.at[0 if way == 0 else height + 1],
            send_sem=edge_send.at[way],
            recv_sem=edge_recv.at[way],
            device_id={"sector": lax.rem(sector + (1 if way == 0 else sectors - 1), sectors)},
            device_id_type=pl.DeviceIdType.MESH,
        )

    def add_halo(way):
        widen_row(x_ref[0 if way == 0 else height + 1], cat_ref, 0)
        row = 1 if way == 0 else height
        sum_ref[row] = sum_ref[row] + jnp.dot(
            cat_ref[0], conv_ref[0 if way == 0 else 2], preferred_element_type=F32
        )

    for c in range(chunks):
        if c == chunks - 1:

            @pl.when(sector < sectors - 1)
            def _():
                edge_copy(1).wait_recv()
                add_halo(1)

        @pl.loop(1, tm_count)
        def _(o):
            back_copy(c, me, lax.rem(me + tm_count - o, tm_count)).wait_recv()

        if c == 0:

            @pl.when(sector > 0)
            def _():
                edge_copy(1).start()

        if c == chunks - 1:

            @pl.when(sector < sectors - 1)
            def _():
                edge_copy(0).start()

        for j in range(tm_count):
            widen_row(x_ref[1 + j * chunks + c], cat_ref, j)
        wide = cat_ref[...].reshape(tm_count * GRID, 3 * channels)
        for r in range(3):
            part = jnp.dot(wide, conv_ref[r], preferred_element_type=F32)
            part = part.reshape(tm_count, GRID, channels)
            for j in range(tm_count):
                row = 2 + j * chunks + c - r
                extra = part[j]
                if r == 1:
                    extra = extra + x_ref[row].astype(F32)
                sum_ref[row] = sum_ref[row] + extra

    @pl.when(sector > 0)
    def _():
        edge_copy(0).wait_recv()
        add_halo(0)

    result_ref[...] = sum_ref[1 : height + 1].reshape(height * GRID, channels).astype(BF)

    @pl.when(sector < sectors - 1)
    def _():
        edge_copy(0).wait_send()

    @pl.when(sector > 0)
    def _():
        edge_copy(1).wait_send()

    @pl.loop(0, chunks)
    def _(c):
        @pl.loop(1, tm_count)
        def _(o):
            target = lax.rem(me + o, tm_count)
            go_copy(c, target, me).wait_send()
            back_copy(c, target, me).wait_send()


def body(
    context, depth_weight, cell_ids, time_embed, norm_gain, w_qkv, w_out, w_up, w_down, conv_weight
):
    tm_count = lax.axis_size("tm")
    sectors = lax.axis_size("sector")
    pixels, channels = context.shape[2:]
    bins = cell_ids.shape[1]
    band = GRID * GRID // sectors
    piece = band // tm_count
    chunk = GRID
    chunks = piece // chunk
    rows = math.gcd(256, tm_count * chunk)
    conv_flat = conv_weight.reshape(3, 3 * channels, channels)
    vmem = pl.BlockSpec(memory_space=pltpu.VMEM)
    anywhere = pl.BlockSpec(memory_space=pl.ANY)
    dma = pltpu.SemaphoreType.DMA
    far = sectors - 1
    result = pl.pallas_call(
        functools.partial(fused_kernel, tm_count, sectors, piece, chunk),
        out_shape=jax.ShapeDtypeStruct((band, channels), BF),
        in_specs=[vmem] * 5 + [anywhere] * 5,
        out_specs=vmem,
        scratch_shapes=[
            pltpu.VMEM(w_qkv.shape, BF),
            pltpu.VMEM(w_out.shape, BF),
            pltpu.VMEM(w_up.shape, BF),
            pltpu.VMEM(w_down.shape, BF),
            pltpu.VMEM(conv_flat.shape, BF),
            pltpu.VMEM((far, pixels, channels), BF),
            pltpu.VMEM((far, bins, pixels), F32),
            pltpu.VMEM((far, bins, pixels), jnp.int32),
            pltpu.VMEM((sectors, bins, LANES16, pixels), BF),
            pltpu.VMEM((sectors, bins, pixels), jnp.int32),
            pltpu.VMEM((bins, LANES16, pixels), BF),
            pltpu.VMEM((rows, pixels), BF),
            pltpu.VMEM((chunks * tm_count, chunk, channels), BF),
            pltpu.VMEM((chunks, tm_count, chunk, channels), BF),
            pltpu.VMEM((chunks, tm_count, chunk, channels), BF),
            pltpu.VMEM((band // GRID + 2, GRID, channels), BF),
            pltpu.VMEM((tm_count, GRID, 3 * channels), BF),
            pltpu.VMEM((band // GRID + 2, GRID, channels), F32),
            dma((5,)),
            dma((far, 3)),
            dma((far, 3)),
            dma((chunks, tm_count)),
            dma((chunks, tm_count)),
            dma((chunks, tm_count)),
            dma((chunks, tm_count)),
            dma((2,)),
            dma((2,)),
        ]
        + encode_scratch(tm_count, chunk, channels),
        compiler_params=pltpu.CompilerParams(
            collective_id=0, has_side_effects=True, vmem_limit_bytes=60 * 2**20
        ),
    )(
        context[0, 0],
        depth_weight[0, 0],
        cell_ids[0],
        time_embed,
        norm_gain,
        w_qkv,
        w_out,
        w_up,
        w_down,
        conv_flat,
    )
    return result.reshape(1, band // GRID, GRID, channels)


def solution(mesh):
    return jax.shard_map(
        body,
        mesh=mesh,
        in_specs=(
            P(("groups", "tm"), "sector", None, None),
            P(("groups", "tm"), "sector", None, None),
            P("sector", None, None),
            P(),
            P(),
            P(),
            P(),
            P(),
            P(),
            P(),
        ),
        out_specs=P(("groups", "tm"), "sector", None, None),
        check_vma=False,
    )
```
